512 devices in a mesh: section: 16 (over y_lo, x, core), expert: 32 (over y_hi, z).
Axes of the slice: x: 4, y: 4 (y_hi: 2, y_lo: 2; y = y_hi * 2 + y_lo), z: 16, core: 2. Of those that a mesh axis runs over, the one named last changes fastest.
Arguments:
- tokens: bfloat16 [8192, 7168], P('expert', 'section'), may hold values from -6 to 6
- grad_out: bfloat16 [8192, 7168], P('expert', 'section'), may hold values from -6 to 6
- expert_ids: int32 [8192, 8], P('expert'), may hold values from 0 to 255, all different within a row; in each aligned block of 256 rows (0 to 255, 256 to 511, ...) at most 12 rows name the same one
- route_weight: float32 [8192, 8], P('expert'), may hold values from 0.1 to 1
- up_weight: bfloat16 [32, 7168, 2048], P('expert', 'section'), may hold values from -0.0625 to 0.0625
- down_weight: bfloat16 [32, 2048, 7168], P('expert', None, 'section'), may hold values from -0.125 to 0.125
Outputs:
- mixed: bfloat16 [8192, 7168], P('expert', 'section')
- grad_tokens: bfloat16 [8192, 7168], P('expert', 'section')
The draws below stay inside these ranges and needn't reach their ends.
Inputs may be any that keep to these rules, and one draw needn't show every extreme that they name: `expert_ids`: in each aligned block of 256 tokens (the rows of one device) no expert number is named by more than 12 routes, and a row names 8 different numbers. Numbers from 32 on belong to experts held elsewhere.
All inputs are finite; a program needn't handle non-finite values.
Results may differ from the reference program's by a relative error of at most 0.029.
Values may be sent and summed in bfloat16 or wider, within the bound.
No kernel may reach another device: no remote copies, remote signals or barrier semaphores. Data moves between devices by JAX's collectives and lax.ppermute only.
A program may use at most 64 MiB of HBM per device.

```python
import math
import jax
import jax.numpy as jnp
import numpy as np
from jax import lax

D = 7168
FF = 2048
EXPERTS_ALL = 256
TOP = 8
TOK_DEV = 256
CAP = 12
EXPERTS = 32
TOKENS = 8192
N_SECTION = 16


def block_scale(key, extent, shards, smallest, top_value):
    gain = 1.0
    for axis_at, shards_of in shards:
        draws = jax.random.uniform(jax.random.fold_in(jax.random.fold_in(key, 6), axis_at), (shards_of,), jnp.float32, smallest / len(shards), top_value / len(shards))
        gain = gain * jnp.repeat(jnp.exp(draws), extent[axis_at] // shards_of).reshape((-1,) + (1,) * (len(extent) - 1 - axis_at))
    return gain


def shared_out(own_key, own, number, rows, amount, top, limit, lean):
    order = jax.random.permutation(own_key, amount)
    crowded, ordinary = shares(amount, rows * top, limit, lean, True), shares(amount, rows * top, limit, lean, False)
    places = jnp.arange(amount)

    def named(tallies, offset_by):
        used = int((tallies > 0).sum())
        fixed = max(1, used // 4)
        passed = fixed + (places - fixed + offset_by * (used - fixed)) % max(1, amount - fixed)
        return jnp.zeros((amount,), jnp.int32).at[order[jnp.where(places < fixed, places, passed)]].set(jnp.asarray(tallies, jnp.int32))

    tallies = jnp.where(number % 4 == 0, named(crowded, number // 4), named(ordinary, number - number // 4 - 1))
    mixed = jax.random.permutation(jax.random.fold_in(own, 3), amount)
    donor, sink = mixed[0:amount // 2 * 2:2], mixed[1:amount // 2 * 2:2]
    slack = jnp.minimum(tallies[donor] - 1, limit - tallies[sink]) // 2
    slack = jnp.where((donor == order[0]) | (sink == order[0]) | (tallies[sink] == 0), 0, jnp.maximum(slack, 0))
    passed = jax.random.randint(jax.random.fold_in(own, 4), (amount // 2,), 0, 1 << 20) % (slack + 1)
    tallies = tallies.at[donor].add(-passed).at[sink].add(passed)
    items = jnp.searchsorted(jnp.cumsum(tallies), jnp.arange(rows * top), side="right").astype(jnp.int32)
    grid = items.reshape(top, rows).T
    grid = grid[jax.random.permutation(jax.random.fold_in(own, 1), rows)]
    offset_by = jax.random.randint(jax.random.fold_in(own, 2), (rows, 1), 0, top)
    return jnp.take_along_axis(grid, (jnp.arange(top)[None, :] + offset_by) % top, axis=1)


def shares(amount, total, bound, skew, full):
    loads = [(1 << 20) // math.isqrt(rank ** skew) + 1 for rank in range(1, amount + 1)]
    largest = bound if full else min(bound, max(-(-total // amount), total * loads[0] // sum(loads)))
    least = 1 if total - largest >= amount - 1 else 0
    counts, spare = [largest] + [least] * (amount - 1), total - largest - least * (amount - 1)
    while spare > 0:
        free = [i for i in range(1, amount) if counts[i] < largest] or [i for i in range(1, amount) if counts[i] < bound]
        mass, remaining = sum([loads[i] for i in free]), spare
        for i in free:
            addition = min(bound - counts[i], max(1, remaining * loads[i] // mass), spare)
            counts[i] = counts[i] + addition
            spare = spare - addition
    return np.array(counts)


def normal_values(stream_key, dims, scale, limit, cuts=(), held_as=jnp.bfloat16):
    drawn = scale * jax.random.normal(stream_key, dims, jnp.float32)
    if cuts:
        drawn = drawn * block_scale(stream_key, dims, cuts, -0.22, 0.18)
    return jnp.clip(drawn, -limit, limit).astype(held_as)


def setup_inputs(seed: int = 0) -> dict:
    key_of = jax.random.split(jax.random.key(seed), 7)
    tokens = normal_values(key_of[0], (TOKENS, D), 1.0, 6.0, ((0, 32), (1, 16)))
    grad_out = normal_values(key_of[1], (TOKENS, D), 1.0, 6.0, ((0, 32), (1, 16)))
    expert_ids_keys = jax.random.split(jax.random.fold_in(key_of[2], 1), TOKENS // TOK_DEV)
    expert_ids_turns = jax.random.permutation(jax.random.fold_in(key_of[2], 3), TOKENS // TOK_DEV)
    expert_ids = jax.vmap(lambda own, number: shared_out(jax.random.fold_in(key_of[2], 2), own, number, TOK_DEV, EXPERTS_ALL, TOP, CAP, 2))(expert_ids_keys, expert_ids_turns).reshape((TOKENS, TOP))
    route_weight = jnp.clip(0.1 + 0.9 * jax.random.uniform(key_of[3], (TOKENS, TOP), jnp.float32) ** block_scale(key_of[3], (TOKENS, TOP), ((0, 32),), -0.2, 0.2), 0.1, 1.0)
    up_weight = normal_values(key_of[4], (EXPERTS, D, FF), D ** -0.5, 0.0625, ((0, 32), (1, 16)))
    down_weight = normal_values(key_of[5], (EXPERTS, FF, D), FF ** -0.5, 0.125, ((0, 32), (2, 16)))
    return {"tokens": tokens, "grad_out": grad_out, "expert_ids": expert_ids, "route_weight": route_weight, "up_weight": up_weight, "down_weight": down_weight}


def slot_tables(expert_ids):
    block_count = expert_ids.shape[0] // TOK_DEV
    route_count = TOK_DEV * TOP
    chosen = expert_ids.reshape(block_count, route_count)
    onehot = (chosen[:, :, None] == jnp.arange(EXPERTS, dtype=jnp.int32)[None, None, :]).astype(jnp.int32)
    before = jnp.sum((jnp.cumsum(onehot, axis=1) - onehot) * onehot, axis=2)
    slot_count = EXPERTS * CAP
    slot = jnp.where(chosen < EXPERTS, chosen * CAP + before, slot_count).astype(jnp.int32)
    table = jnp.full((block_count, slot_count + 1), route_count, jnp.int32)
    routes_all = jnp.broadcast_to(jnp.arange(route_count, dtype=jnp.int32)[None, :], (block_count, route_count))
    table = table.at[jnp.arange(block_count, dtype=jnp.int32)[:, None], slot].set(routes_all)
    return slot, table[:, :slot_count]


def section_sum(pieces):
    rounded = lax.optimization_barrier(pieces.astype(jnp.bfloat16))
    return jnp.sum(rounded.astype(jnp.float32), axis=0)


def expert_pass(item):
    rows_x, rows_dy, up_matrix, down_matrix = item
    row_count = rows_x.shape[0]
    width = D // N_SECTION
    pieces = jnp.einsum("rsd,sdf->srf", rows_x.reshape(row_count, N_SECTION, width).astype(jnp.float32),
                        up_matrix.reshape(N_SECTION, width, FF).astype(jnp.float32))
    pre = section_sum(pieces)
    hidden = jax.nn.silu(pre).astype(jnp.bfloat16)
    rows_y = jnp.dot(hidden, down_matrix, preferred_element_type=jnp.float32).astype(jnp.bfloat16)
    back_pieces = jnp.einsum("rsd,fsd->srf", rows_dy.reshape(row_count, N_SECTION, width).astype(jnp.float32),
                             down_matrix.reshape(FF, N_SECTION, width).astype(jnp.float32))
    dhid = section_sum(back_pieces)
    sigma = jax.nn.sigmoid(pre)
    dpre = (dhid * sigma * (1.0 + pre * (1.0 - sigma))).astype(jnp.bfloat16)
    rows_dx = jnp.dot(dpre, up_matrix.T, preferred_element_type=jnp.float32).astype(jnp.bfloat16)
    return rows_y, rows_dx


def combine(item):
    back_y, back_dx, slot, weights = item
    zero_row = jnp.zeros((1, D), jnp.bfloat16)
    y_padded = jnp.concatenate([back_y, zero_row], axis=0)
    dx_padded = jnp.concatenate([back_dx, zero_row], axis=0)
    picked_y = y_padded[slot].reshape(TOK_DEV, TOP, D).astype(jnp.float32)
    picked_dx = dx_padded[slot].reshape(TOK_DEV, TOP, D).astype(jnp.float32)
    mixed = jnp.sum(picked_y * weights[:, :, None], axis=1).astype(jnp.bfloat16)
    grad = jnp.sum(picked_dx, axis=1).astype(jnp.bfloat16)
    return mixed, grad


def reference(tokens, grad_out, expert_ids, route_weight, up_weight, down_weight):
    block_count = tokens.shape[0] // TOK_DEV
    slot, table = slot_tables(expert_ids)
    token_of = table // TOP
    zero_rows = jnp.zeros((block_count, 1, D), jnp.bfloat16)
    tok_padded = jnp.concatenate([tokens.reshape(block_count, TOK_DEV, D), zero_rows], axis=1)
    grad_padded = jnp.concatenate([grad_out.reshape(block_count, TOK_DEV, D), zero_rows], axis=1)
    gate_padded = jnp.concatenate([route_weight.reshape(block_count, TOK_DEV * TOP),
                                   jnp.zeros((block_count, 1), jnp.float32)], axis=1)
    block_index = jnp.arange(block_count, dtype=jnp.int32)[:, None]
    sent_x = tok_padded[block_index, token_of]
    slot_gate = gate_padded[block_index, table]
    sent_dy = (slot_gate[:, :, None] * grad_padded[block_index, token_of].astype(jnp.float32)).astype(jnp.bfloat16)
    by_expert_x = sent_x.reshape(block_count, EXPERTS, CAP, D).transpose(1, 0, 2, 3).reshape(EXPERTS, block_count * CAP, D)
    by_expert_dy = sent_dy.reshape(block_count, EXPERTS, CAP, D).transpose(1, 0, 2, 3).reshape(EXPERTS, block_count * CAP, D)
    rows_y, rows_dx = lax.map(expert_pass, (by_expert_x, by_expert_dy, up_weight, down_weight))
    back_y = rows_y.reshape(EXPERTS, block_count, CAP, D).transpose(1, 0, 2, 3).reshape(block_count, EXPERTS * CAP, D)
    back_dx = rows_dx.reshape(EXPERTS, block_count, CAP, D).transpose(1, 0, 2, 3).reshape(block_count, EXPERTS * CAP, D)
    mixed, grad = lax.map(combine, (back_y, back_dx, slot, route_weight.reshape(block_count, TOK_DEV, TOP)))
    return mixed.reshape(block_count * TOK_DEV, D), grad.reshape(block_count * TOK_DEV, D)
```

```python
import jax
import jax.numpy as jnp
from jax import lax
from jax.experimental import pallas as pl
from jax.experimental.pallas import tpu as pltpu
from jax.sharding import PartitionSpec as P

CAP = 12
HALF = CAP // 2
TILES = 11
SHIFTS = ((0, 0, 0), (-6, 0, 1), (2, 1, 1), (-4, 1, 2), (4, 2, 2), (-2, 2, 3))
F32 = jnp.float32
BF16 = jnp.bfloat16


def pairs_of(first_tile, first_group):
    return [
        (first_tile + 3 * n, first_group + 4 * n)
        for n in range(4)
        if first_tile + 3 * n < TILES and first_group + 4 * n < 14
    ]


def dot(a, b, contract):
    return lax.dot_general(a, b, ((contract[0], contract[1]), ((), ())), preferred_element_type=F32)


def placed(rank3, shift):
    experts, _, tokens = rank3.shape
    row = lax.broadcasted_iota(jnp.int32, rank3.shape, 1).astype(F32) + float(shift)
    return jnp.where(rank3 == row, 1.0, 0.0).reshape(experts * 8, tokens)


def route(ids, gates, core, experts):
    tokens = ids.shape[1]
    expert_row = lax.broadcasted_iota(jnp.int32, (experts, tokens), 0)
    named = jnp.zeros((experts, tokens), F32)
    gate = jnp.zeros((experts, tokens), F32)
    for k in range(ids.shape[0]):
        hit = ids[k : k + 1, :] == expert_row
        named = named + jnp.where(hit, 1.0, 0.0)
        gate = gate + jnp.where(hit, gates[k : k + 1, :], 0.0)
    earlier = lax.broadcasted_iota(jnp.int32, (tokens, tokens), 0) < lax.broadcasted_iota(
        jnp.int32, (tokens, tokens), 1
    )
    before = dot(named.astype(BF16), jnp.where(earlier, 1.0, 0.0).astype(BF16), ((1,), (0,)))
    rank = before - core * float(HALF)
    kept = (named > 0.5) & (rank > -0.5) & (rank < HALF - 0.5)
    return jnp.where(kept, rank, -100.0), gate


def pack_rows(rank, gate, source):
    experts, tokens = rank.shape
    rank3 = jnp.broadcast_to(rank[:, None, :], (experts, 8, tokens))
    gate2 = jnp.broadcast_to(gate[:, None, :], (experts, 8, tokens)).reshape(experts * 8, tokens)
    tiles = [None] * TILES
    for shift, tile, group in SHIFTS:
        pairs = pairs_of(tile, group)
        onehot = placed(rank3, shift)
        weight = jnp.sum(onehot * gate2, axis=1, keepdims=True)
        stacked = jnp.concatenate([source[g] for _, g in pairs], axis=0)
        rows = dot(onehot.astype(BF16), stacked, ((1,), (1,)))
        for n, (k, g) in enumerate(pairs):
            part = rows[:, n * 128 : (n + 1) * 128]
            part = part if g < 7 else part * weight
            tiles[k] = part if tiles[k] is None else tiles[k] + part
    return jnp.concatenate([t.reshape(experts, 8, 128) for t in tiles], axis=1)


def split_tiles(message):
    blocks = message.shape[0]
    wide = message.astype(F32).reshape(blocks, TILES, 8, 128)
    return [wide[:, k].reshape(blocks * 8, 128).astype(BF16) for k in range(TILES)]


def chosen_rows(blocks, shift, flipped):
    shape = (blocks * 8, blocks * HALF) if flipped else (blocks * HALF, blocks * 8)
    compact = lax.broadcasted_iota(jnp.int32, shape, 1 if flipped else 0)
    packed = lax.broadcasted_iota(jnp.int32, shape, 0 if flipped else 1)
    bits = blocks.bit_length() - 1
    same = (packed >> 3 == (compact & (blocks - 1))) & ((packed & 7) + shift == compact >> bits)
    return jnp.where(same, 1.0, 0.0).astype(BF16)


def unpack_rows(tiles, blocks):
    groups = [None] * 14
    for shift, tile, group in SHIFTS:
        pairs = pairs_of(tile, group)
        stacked = jnp.concatenate([tiles[k] for k, _ in pairs], axis=1)
        rows = dot(chosen_rows(blocks, shift, False), stacked, ((1,), (0,)))
        for n, (k, g) in enumerate(pairs):
            part = rows[:, n * 128 : (n + 1) * 128]
            groups[g] = part if groups[g] is None else groups[g] + part
    return groups


def repack_rows(groups, blocks):
    tiles = [None] * TILES
    for shift, tile, group in SHIFTS:
        pairs = pairs_of(tile, group)
        stacked = jnp.concatenate([groups[g] for _, g in pairs], axis=1)
        rows = dot(chosen_rows(blocks, shift, True), stacked, ((1,), (0,)))
        for n, (k, g) in enumerate(pairs):
            part = rows[:, n * 128 : (n + 1) * 128]
            tiles[k] = part if tiles[k] is None else tiles[k] + part
    return jnp.concatenate([t.reshape(blocks, 8, 128) for t in tiles], axis=1)


def combine_rows(rank, gate, tiles):
    experts, tokens = rank.shape
    rank3 = jnp.broadcast_to(rank[:, None, :], (experts, 8, tokens))
    gate2 = jnp.broadcast_to(gate[:, None, :], (experts, 8, tokens)).reshape(experts * 8, tokens)
    groups = [None] * 14

    def add(g, part):
        groups[g] = part if groups[g] is None else groups[g] + part

    for shift, tile, group in SHIFTS:
        pairs = pairs_of(tile, group)
        onehot = placed(rank3, shift)
        weight = onehot * gate2
        high = weight.astype(BF16)
        low = (weight - high.astype(F32)).astype(BF16)
        for scaled in (True, False):
            some = [(k, g) for k, g in pairs if (g < 7) == scaled]
            stacked = jnp.concatenate([tiles[k] for k, _ in some], axis=1)
            if scaled:
                sums = dot(stacked, high, ((0,), (0,))) + dot(stacked, low, ((0,), (0,)))
            else:
                sums = dot(stacked, onehot.astype(BF16), ((0,), (0,)))
            for n, (_, g) in enumerate(some):
                add(g, sums[n * 128 : (n + 1) * 128])
    return jnp.concatenate(groups[:7], axis=0), jnp.concatenate(groups[7:], axis=0)


def send_kernel(core_ref, ids_ref, gates_ref, tok_a, tok_b, dy_a, dy_b, out_ref, rank_ref, gate_ref):
    experts = out_ref.shape[0]
    rank, gate = route(ids_ref[...], gates_ref[...], core_ref[0, 0].astype(F32), experts)
    rank_ref[...] = rank
    gate_ref[...] = gate
    feats = jnp.concatenate([tok_a[...], tok_b[...], dy_a[...], dy_b[...]], axis=0)
    source = [feats[g * 128 : (g + 1) * 128] for g in range(14)]
    out_ref[...] = pack_rows(rank, gate, source).astype(BF16)


def up_kernel(recv_ref, up_a, up_b, down_a, down_b, out_ref, x_ref, dy_ref):
    @pl.when(pl.program_id(0) == 0)
    def _():
        blocks = recv_ref.shape[0]
        groups = unpack_rows(split_tiles(recv_ref[...]), blocks)
        for g in range(7):
            x_ref[:, g * 128 : (g + 1) * 128] = groups[g].astype(BF16)
            dy_ref[:, g * 128 : (g + 1) * 128] = groups[7 + g].astype(BF16)

    rows = x_ref.shape[0]
    up = jnp.concatenate([up_a[...], up_b[...]], axis=0)
    down = jnp.concatenate([down_a[...], down_b[...]], axis=0)
    out_ref[0, :rows, :] = dot(x_ref[...], up, ((1,), (0,))).astype(BF16)
    out_ref[0, rows:, :] = dot(dy_ref[...], down, ((1,), (0,))).astype(BF16)


def act_kernel(parts_ref, out_ref):
    summed = jnp.sum(parts_ref[...].astype(F32), axis=0)
    pre = summed[0]
    dhid = summed[1]
    sigma = 1.0 / (1.0 + jnp.exp(-pre))
    hidden = (pre * sigma).astype(BF16)
    dpre = (dhid * sigma * (1.0 + pre * (1.0 - sigma))).astype(BF16)
    for q in range(out_ref.shape[0]):
        out_ref[q, 0] = hidden
        out_ref[q, 1] = dpre


def down_kernel(recv_ref, up_a, up_b, down_a, down_b, out_ref, y_ref, dx_ref):
    step = pl.program_id(0)
    rows = y_ref.shape[0]
    up = jnp.concatenate([up_a[...], up_b[...]], axis=0)
    down = jnp.concatenate([down_a[...], down_b[...]], axis=0)
    y = dot(recv_ref[0, :rows, :], down, ((1,), (1,)))
    dx = dot(recv_ref[0, rows:, :], up, ((1,), (1,)))

    @pl.when(step == 0)
    def _():
        y_ref[...] = y
        dx_ref[...] = dx

    @pl.when(step > 0)
    def _():
        y_ref[...] += y
        dx_ref[...] += dx

    @pl.when(step == pl.num_programs(0) - 1)
    def _():
        blocks = out_ref.shape[0]
        groups = [ref[:, g * 128 : (g + 1) * 128].astype(BF16) for ref in (y_ref, dx_ref) for g in range(7)]
        out_ref[...] = repack_rows(groups, blocks).astype(BF16)


def combine_kernel(rank_ref, gate_ref, recv_ref, mixed_ref, grad_ref, other_ref):
    mixed, grad = combine_rows(rank_ref[...], gate_ref[...], split_tiles(recv_ref[...]))
    width = mixed_ref.shape[0]
    mixed_ref[...] = mixed[:width]
    grad_ref[...] = grad[:width]
    other_ref[0] = mixed[width:].astype(BF16)
    other_ref[1] = grad[width:].astype(BF16)


def params():
    return pltpu.CompilerParams(vmem_limit_bytes=40 * 1024 * 1024)


def whole(shape):
    return pl.BlockSpec(shape, lambda *_: (0,) * len(shape))


def local(tokens, grad_out, expert_ids, route_weight, up_weight, down_weight):
    tok_count, features = tokens.shape
    experts = lax.axis_size("expert")
    sections = lax.axis_size("section")
    chips = sections // 2
    hidden_units = up_weight.shape[2]
    block = hidden_units // chips
    rows = experts * HALF
    swap = [(s, s ^ 1) for s in range(sections)]
    same_core = [[2 * q + c for q in range(chips)] for c in range(2)]
    core = (lax.axis_index("section") & 1).astype(jnp.int32).reshape(1, 1)

    tok_a, dy_a = tokens.T, grad_out.T
    tok_b, dy_b = lax.ppermute(tok_a, "section", swap), lax.ppermute(dy_a, "section", swap)
    message = jax.ShapeDtypeStruct((experts, 8 * TILES, 128), BF16)
    by_expert = jax.ShapeDtypeStruct((experts, tok_count), F32)
    send, rank, gate = pl.pallas_call(
        send_kernel,
        out_shape=(message, by_expert, by_expert),
        in_specs=[pl.BlockSpec(memory_space=pltpu.SMEM)] + [pl.BlockSpec(memory_space=pltpu.VMEM)] * 6,
        out_specs=[pl.BlockSpec(memory_space=pltpu.VMEM)] * 3,
        compiler_params=params(),
        name="send_rows",
    )(core, expert_ids.T, route_weight.T, tok_a, tok_b, dy_a, dy_b)
    recv = lax.all_to_all(send, "expert", split_axis=0, concat_axis=0, tiled=True)

    up_a, down_a = up_weight[0], down_weight[0].T
    up_b, down_b = lax.ppermute(up_a, "section", swap), lax.ppermute(down_a, "section", swap)
    weights = (up_a, up_b, down_a, down_b)
    weight_specs = [pl.BlockSpec((features, block), lambda q: (0, q))] * 4
    parts = pl.pallas_call(
        up_kernel,
        grid=(chips,),
        out_shape=jax.ShapeDtypeStruct((chips, 2 * rows, block), BF16),
        in_specs=[whole(message.shape)] + weight_specs,
        out_specs=pl.BlockSpec((1, 2 * rows, block), lambda q: (q, 0, 0)),
        scratch_shapes=[pltpu.VMEM((rows, 2 * features), BF16)] * 2,
        compiler_params=params(),
        name="up_products",
    )(recv, *weights)
    parts = lax.all_to_all(
        parts, "section", split_axis=0, concat_axis=0, axis_index_groups=same_core, tiled=True
    )
    steps = 4
    act_spec = pl.BlockSpec((chips, 2, rows // steps, block), lambda i: (0, 0, i, 0))
    acts = pl.pallas_call(
        act_kernel,
        grid=(steps,),
        out_shape=jax.ShapeDtypeStruct((chips, 2, rows, block), BF16),
        in_specs=[act_spec],
        out_specs=act_spec,
        compiler_params=params(),
        name="activations",
    )(parts.reshape(chips, 2, rows, block))
    acts = lax.all_to_all(
        acts.reshape(chips, 2 * rows, block),
        "section",
        split_axis=0,
        concat_axis=0,
        axis_index_groups=same_core,
        tiled=True,
    )
    back = pl.pallas_call(
        down_kernel,
        grid=(chips,),
        out_shape=message,
        in_specs=[pl.BlockSpec((1, 2 * rows, block), lambda q: (q, 0, 0))] + weight_specs,
        out_specs=whole(message.shape),
        scratch_shapes=[pltpu.VMEM((rows, 2 * features), F32)] * 2,
        compiler_params=params(),
        name="down_products",
    )(acts, *weights)
    back = lax.all_to_all(back, "expert", split_axis=0, concat_axis=0, tiled=True)
    own = jax.ShapeDtypeStruct((features, tok_count), F32)
    mixed, grad, other = pl.pallas_call(
        combine_kernel,
        out_shape=(own, own, jax.ShapeDtypeStruct((2, features, tok_count), BF16)),
        in_specs=[pl.BlockSpec(memory_space=pltpu.VMEM)] * 3,
        out_specs=[pl.BlockSpec(memory_space=pltpu.VMEM)] * 3,
        compiler_params=params(),
        name="combine_rows",
    )(rank, gate, back)
    other = lax.ppermute(other, "section", swap).astype(F32)
    return (mixed + other[0]).astype(BF16).T, (grad + other[1]).astype(BF16).T


def solution(mesh):
    return jax.shard_map(
        local,
        mesh=mesh,
        in_specs=(
            P("expert", "section"),
            P("expert", "section"),
            P("expert", None),
            P("expert", None),
            P("expert", "section", None),
            P("expert", None, "section"),
        ),
        out_specs=(P("expert", "section"), P("expert", "section")),
        check_vma=False,
    )
```

```python
import jax
import jax.numpy as jnp
from jax import lax
from jax.experimental import pallas as pl
from jax.experimental.pallas import tpu as pltpu
from jax.sharding import PartitionSpec as P

CAP = 12
LEAD = 8
HALF = CAP // 2
TILES = 11
SHIFTS = ((0, 0, 0), (-6, 0, 1), (2, 1, 1), (-4, 1, 2), (4, 2, 2), (-2, 2, 3))
F32 = jnp.float32
BF16 = jnp.bfloat16


def pairs_of(first_tile, first_group):
    return [
        (first_tile + 3 * n, first_group + 4 * n)
        for n in range(4)
        if first_tile + 3 * n < TILES and first_group + 4 * n < 14
    ]


def dot(a, b, contract):
    return lax.dot_general(a, b, ((contract[0], contract[1]), ((), ())), preferred_element_type=F32)


def placed(rank3, shift):
    experts, _, tokens = rank3.shape
    row = lax.broadcasted_iota(jnp.int32, rank3.shape, 1).astype(F32) + float(shift)
    return jnp.where(rank3 == row, 1.0, 0.0).reshape(experts * 8, tokens)


def route(ids, gates, core, experts):
    tokens = ids.shape[1]
    expert_row = lax.broadcasted_iota(jnp.int32, (experts, tokens), 0)
    named = jnp.zeros((experts, tokens), F32)
    gate = jnp.zeros((experts, tokens), F32)
    for k in range(ids.shape[0]):
        hit = ids[k : k + 1, :] == expert_row
        named = named + jnp.where(hit, 1.0, 0.0)
        gate = gate + jnp.where(hit, gates[k : k + 1, :], 0.0)
    earlier = lax.broadcasted_iota(jnp.int32, (tokens, tokens), 0) < lax.broadcasted_iota(
        jnp.int32, (tokens, tokens), 1
    )
    before = dot(named.astype(BF16), jnp.where(earlier, 1.0, 0.0).astype(BF16), ((1,), (0,)))
    rank = before - core * float(HALF)
    kept = (named > 0.5) & (rank > -0.5) & (rank < HALF - 0.5)
    return jnp.where(kept, rank, -100.0), gate


def pack_rows(rank, gate, source):
    experts, tokens = rank.shape
    rank3 = jnp.broadcast_to(rank[:, None, :], (experts, 8, tokens))
    gate2 = jnp.broadcast_to(gate[:, None, :], (experts, 8, tokens)).reshape(experts * 8, tokens)
    tiles = [None] * TILES
    for shift, tile, group in SHIFTS:
        pairs = pairs_of(tile, group)
        onehot = placed(rank3, shift)
        weight = jnp.sum(onehot * gate2, axis=1, keepdims=True)
        stacked = jnp.concatenate([source[g] for _, g in pairs], axis=0)
        rows = dot(onehot.astype(BF16), stacked, ((1,), (1,)))
        for n, (k, g) in enumerate(pairs):
            part = rows[:, n * 128 : (n + 1) * 128]
            part = part if g < 7 else part * weight
            tiles[k] = part if tiles[k] is None else tiles[k] + part
    return jnp.concatenate([t.reshape(experts, 8, 128) for t in tiles], axis=1)


def split_tiles(message):
    blocks = message.shape[0]
    wide = message.astype(F32).reshape(blocks, TILES, 8, 128)
    return [wide[:, k].reshape(blocks * 8, 128).astype(BF16) for k in range(TILES)]


def chosen_rows(blocks, shift, flipped):
    shape = (blocks * 8, blocks * HALF) if flipped else (blocks * HALF, blocks * 8)
    compact = lax.broadcasted_iota(jnp.int32, shape, 1 if flipped else 0)
    packed = lax.broadcasted_iota(jnp.int32, shape, 0 if flipped else 1)
    bits = blocks.bit_length() - 1
    same = (packed >> 3 == (compact & (blocks - 1))) & ((packed & 7) + shift == compact >> bits)
    return jnp.where(same, 1.0, 0.0).astype(BF16)


def unpack_rows(tiles, blocks):
    groups = [None] * 14
    for shift, tile, group in SHIFTS:
        pairs = pairs_of(tile, group)
        stacked = jnp.concatenate([tiles[k] for k, _ in pairs], axis=1)
        rows = dot(chosen_rows(blocks, shift, False), stacked, ((1,), (0,)))
        for n, (k, g) in enumerate(pairs):
            part = rows[:, n * 128 : (n + 1) * 128]
            groups[g] = part if groups[g] is None else groups[g] + part
    return groups


def repack_rows(groups, blocks):
    tiles = [None] * TILES
    for shift, tile, group in SHIFTS:
        pairs = pairs_of(tile, group)
        stacked = jnp.concatenate([groups[g] for _, g in pairs], axis=1)
        rows = dot(chosen_rows(blocks, shift, True), stacked, ((1,), (0,)))
        for n, (k, g) in enumerate(pairs):
            part = rows[:, n * 128 : (n + 1) * 128]
            tiles[k] = part if tiles[k] is None else tiles[k] + part
    return jnp.concatenate([t.reshape(blocks, 8, 128) for t in tiles], axis=1)


def combine_rows(rank, gate, tiles):
    experts, tokens = rank.shape
    rank3 = jnp.broadcast_to(rank[:, None, :], (experts, 8, tokens))
    gate2 = jnp.broadcast_to(gate[:, None, :], (experts, 8, tokens)).reshape(experts * 8, tokens)
    groups = [None] * 14

    def add(g, part):
        groups[g] = part if groups[g] is None else groups[g] + part

    for shift, tile, group in SHIFTS:
        pairs = pairs_of(tile, group)
        onehot = placed(rank3, shift)
        weight = onehot * gate2
        high = weight.astype(BF16)
        low = (weight - high.astype(F32)).astype(BF16)
        for scaled in (True, False):
            some = [(k, g) for k, g in pairs if (g < 7) == scaled]
            stacked = jnp.concatenate([tiles[k] for k, _ in some], axis=1)
            if scaled:
                sums = dot(stacked, high, ((0,), (0,))) + dot(stacked, low, ((0,), (0,)))
            else:
                sums = dot(stacked, onehot.astype(BF16), ((0,), (0,)))
            for n, (_, g) in enumerate(some):
                add(g, sums[n * 128 : (n + 1) * 128])
    return jnp.concatenate(groups[:7], axis=0), jnp.concatenate(groups[7:], axis=0)


def route_kernel(core_ref, ids_ref, gates_ref, rank_ref, gate_ref):
    core = core_ref[0, 0].astype(F32)
    rank_ref[...], gate_ref[...] = route(ids_ref[...], gates_ref[...], core, rank_ref.shape[0])


def send_kernel(rank_ref, gate_ref, own_ref, other_ref, out_ref):
    half = own_ref.shape[0] // 2
    feats = jnp.concatenate(
        [own_ref[:half, :], other_ref[:half, :], own_ref[half:, :], other_ref[half:, :]], axis=0
    )
    source = [feats[g * 128 : (g + 1) * 128] for g in range(14)]
    out_ref[...] = pack_rows(rank_ref[...], gate_ref[...], source).astype(BF16)


def up_kernel(
    recv_ref, up_own, up_other, down_own, down_other, out_ref, up_ref, down_ref, x_ref, dy_ref, sems
):
    features = up_own.shape[0]
    copies = []
    for i, (ref, joined) in enumerate(
        ((up_own, up_ref), (up_other, up_ref), (down_own, down_ref), (down_other, down_ref))
    ):
        held = joined.at[pl.ds((i % 2) * features, features), :]
        copies.append(pltpu.make_async_copy(ref, held, sems.at[i]))
    for copy in copies:
        copy.start()
    groups = unpack_rows(split_tiles(recv_ref[...]), recv_ref.shape[0])
    for g in range(7):
        x_ref[:, g * 128 : (g + 1) * 128] = groups[g].astype(BF16)
        dy_ref[:, g * 128 : (g + 1) * 128] = groups[7 + g].astype(BF16)
    rows = x_ref.shape[0]
    block = out_ref.shape[2]
    for n, (lhs, joined) in enumerate(((x_ref, up_ref), (dy_ref, down_ref))):
        copies[2 * n].wait()
        copies[2 * n + 1].wait()
        for q in range(out_ref.shape[0]):
            units = slice(q * block, (q + 1) * block)
            part = dot(lhs[...], joined[:, units], ((1,), (0,)))
            out_ref[q, n * rows : (n + 1) * rows, :] = part.astype(BF16)


def act_kernel(parts_ref, out_ref):
    summed = jnp.sum(parts_ref[...].astype(F32), axis=0)
    pre = summed[0]
    dhid = summed[1]
    sigma = 1.0 / (1.0 + jnp.exp(-pre))
    hidden = (pre * sigma).astype(BF16)
    dpre = (dhid * sigma * (1.0 + pre * (1.0 - sigma))).astype(BF16)
    for q in range(out_ref.shape[0]):
        out_ref[q, 0] = hidden
        out_ref[q, 1] = dpre


def down_kernel(recv_ref, up_ref, down_ref, out_ref):
    chips, rows, _ = recv_ref.shape
    half = rows // 2
    features = up_ref.shape[0]
    groups = []
    for first, weight_ref in ((0, down_ref), (half, up_ref)):
        acts = jnp.concatenate([recv_ref[q, first : first + half, :] for q in range(chips)], axis=1)
        for start in range(0, features, 256):
            stop = min(start + 256, features)
            out = dot(acts, weight_ref[start:stop, :], ((1,), (1,))).astype(BF16)
            groups += [out[:, n : n + 128] for n in range(0, stop - start, 128)]
    out_ref[...] = repack_rows(groups, out_ref.shape[0]).astype(BF16)


def combine_kernel(rank_ref, gate_ref, recv_ref, mixed_ref, grad_ref, other_ref):
    mixed, grad = combine_rows(rank_ref[...], gate_ref[...], split_tiles(recv_ref[...]))
    width = mixed_ref.shape[0]
    mixed_ref[...] = mixed[:width]
    grad_ref[...] = grad[:width]
    other_ref[0] = mixed[width:].astype(BF16)
    other_ref[1] = grad[width:].astype(BF16)


def in_vmem(kernel, name, outs, operands, far=(), scratch=(), mebibytes=16):
    vmem = pl.BlockSpec(memory_space=pltpu.VMEM)
    scalar = pl.BlockSpec(memory_space=pltpu.SMEM)
    hbm = pl.BlockSpec(memory_space=pltpu.HBM)
    return pl.pallas_call(
        kernel,
        out_shape=outs,
        in_specs=[scalar if x.size == 1 else vmem for x in operands] + [hbm] * len(far),
        out_specs=jax.tree.map(lambda _: vmem, outs),
        scratch_shapes=list(scratch),
        compiler_params=pltpu.CompilerParams(vmem_limit_bytes=mebibytes * 1024 * 1024),
        name=name,
    )(*operands, *far)


def local(tokens, grad_out, expert_ids, route_weight, up_weight, down_weight):
    tok_count, features = tokens.shape
    experts = lax.axis_size("expert")
    sections = lax.axis_size("section")
    chips = sections // 2
    hidden_units = up_weight.shape[2]
    block = hidden_units // chips
    rows = experts * HALF
    swap = [(s, s ^ 1) for s in range(sections)]
    same_core = [[2 * q + c for q in range(chips)] for c in range(2)]
    core = (lax.axis_index("section") & 1).astype(jnp.int32).reshape(1, 1)
    message = jax.ShapeDtypeStruct((experts, 8 * TILES, 128), BF16)
    by_expert = jax.ShapeDtypeStruct((experts, tok_count), F32)
    parts_type = jax.ShapeDtypeStruct((chips, 2 * rows, block), BF16)

    def across_experts(x):
        return lax.all_to_all(x, "expert", split_axis=0, concat_axis=0, tiled=True)

    def across_chips(x):
        return lax.all_to_all(
            x, "section", split_axis=0, concat_axis=0, axis_index_groups=same_core, tiled=True
        )

    own = jnp.concatenate([tokens.T, grad_out.T], axis=0)
    other = lax.ppermute(own, "section", swap)
    rank, gate = in_vmem(
        route_kernel, "route", (by_expert, by_expert), (core, expert_ids.T, route_weight.T)
    )
    up_own, down_own = up_weight[0], down_weight[0].T
    up_other = lax.ppermute(up_own, "section", swap)
    down_other = lax.ppermute(down_own, "section", swap)

    def at_once(rows):
        return across_experts(rows)

    def in_two(rows):
        return jnp.concatenate([across_experts(rows[:, :LEAD]), across_experts(rows[:, LEAD:])], axis=1)

    send = in_vmem(send_kernel, "send_rows", message, (rank, gate, own, other))
    recv = lax.cond(core[0, 0] == 0, at_once, in_two, send)

    joined = jax.ShapeDtypeStruct((2 * features, hidden_units), BF16)
    parts, up_both, down_both = in_vmem(
        up_kernel,
        "up_products",
        (parts_type, joined, joined),
        (recv,),
        (up_own, up_other, down_own, down_other),
        [pltpu.VMEM((rows, 2 * features), BF16)] * 2 + [pltpu.SemaphoreType.DMA((4,))],
        44,
    )
    parts = across_chips(parts)
    steps = 4
    act_spec = pl.BlockSpec((chips, 2, rows // steps, block), lambda i: (0, 0, i, 0))
    acts = pl.pallas_call(
        act_kernel,
        grid=(steps,),
        out_shape=jax.ShapeDtypeStruct((chips, 2, rows, block), BF16),
        in_specs=[act_spec],
        out_specs=act_spec,
        compiler_params=pltpu.CompilerParams(vmem_limit_bytes=16 * 1024 * 1024),
        name="activations",
    )(parts.reshape(chips, 2, rows, block))
    acts = across_chips(acts.reshape(chips, 2 * rows, block))
    back = across_experts(in_vmem(down_kernel, "down_products", message, (acts, up_both, down_both)))

    own_sum = jax.ShapeDtypeStruct((features, tok_count), F32)
    mixed, grad, rest = in_vmem(
        combine_kernel,
        "combine_rows",
        (own_sum, own_sum, jax.ShapeDtypeStruct((2, features, tok_count), BF16)),
        (rank, gate, back),
    )
    rest = lax.ppermute(rest, "section", swap).astype(F32)
    return (mixed + rest[0]).astype(BF16).T, (grad + rest[1]).astype(BF16).T


def solution(mesh):
    return jax.shard_map(
        local,
        mesh=mesh,
        in_specs=(
            P("expert", "section"),
            P("expert", "section"),
            P("expert", None),
            P("expert", None),
            P("expert", "section", None),
            P("expert", None, "section"),
        ),
        out_specs=(P("expert", "section"), P("expert", "section")),
        check_vma=False,
    )
```

```python
import functools

import jax
import jax.numpy as jnp
from jax import lax
from jax.experimental import pallas as pl
from jax.experimental.pallas import tpu as pltpu
from jax.sharding import PartitionSpec as P

CAP = 12
LEAD = 8
HALF = CAP // 2
TILES = 11
SHIFTS = ((0, 0, 0), (-6, 0, 1), (2, 1, 1), (-4, 1, 2), (4, 2, 2), (-2, 2, 3))
F32 = jnp.float32
BF16 = jnp.bfloat16


def pairs_of(first_tile, first_group):
    return [
        (first_tile + 3 * n, first_group + 4 * n)
        for n in range(4)
        if first_tile + 3 * n < TILES and first_group + 4 * n < 14
    ]


def dot(a, b, contract):
    return lax.dot_general(a, b, ((contract[0], contract[1]), ((), ())), preferred_element_type=F32)


def placed(rank3, shift):
    experts, _, tokens = rank3.shape
    row = lax.broadcasted_iota(jnp.int32, rank3.shape, 1).astype(F32) + float(shift)
    return jnp.where(rank3 == row, 1.0, 0.0).reshape(experts * 8, tokens)


def route(ids, gates, core, experts):
    tokens = ids.shape[1]
    expert_row = lax.broadcasted_iota(jnp.int32, (experts, tokens), 0)
    named = jnp.zeros((experts, tokens), F32)
    gate = jnp.zeros((experts, tokens), F32)
    for k in range(ids.shape[0]):
        hit = ids[k : k + 1, :] == expert_row
        named = named + jnp.where(hit, 1.0, 0.0)
        gate = gate + jnp.where(hit, gates[k : k + 1, :], 0.0)
    earlier = lax.broadcasted_iota(jnp.int32, (tokens, tokens), 0) < lax.broadcasted_iota(
        jnp.int32, (tokens, tokens), 1
    )
    before = dot(named.astype(BF16), jnp.where(earlier, 1.0, 0.0).astype(BF16), ((1,), (0,)))
    rank = before - core * float(HALF)
    kept = (named > 0.5) & (rank > -0.5) & (rank < HALF - 0.5)
    return jnp.where(kept, rank, -100.0), gate


def pack_rows(rank, gate, source):
    experts, tokens = rank.shape
    rank3 = jnp.broadcast_to(rank[:, None, :], (experts, 8, tokens))
    gate2 = jnp.broadcast_to(gate[:, None, :], (experts, 8, tokens)).reshape(experts * 8, tokens)
    tiles = [None] * TILES
    for shift, tile, group in SHIFTS:
        pairs = pairs_of(tile, group)
        onehot = placed(rank3, shift)
        weight = jnp.sum(onehot * gate2, axis=1, keepdims=True)
        stacked = jnp.concatenate([source[g] for _, g in pairs], axis=0)
        rows = dot(onehot.astype(BF16), stacked, ((1,), (1,)))
        for n, (k, g) in enumerate(pairs):
            part = rows[:, n * 128 : (n + 1) * 128]
            part = part if g < 7 else part * weight
            tiles[k] = part if tiles[k] is None else tiles[k] + part
    return jnp.concatenate([t.reshape(experts, 8, 128) for t in tiles], axis=1)


def split_tiles(message):
    blocks, rows, _ = message.shape
    wide = message.astype(F32).reshape(blocks, rows // 8, 8, 128)
    return [wide[:, k].reshape(blocks * 8, 128).astype(BF16) for k in range(rows // 8)]


def chosen_rows(blocks, shift, flipped):
    shape = (blocks * 8, blocks * HALF) if flipped else (blocks * HALF, blocks * 8)
    compact = lax.broadcasted_iota(jnp.int32, shape, 1 if flipped else 0)
    packed = lax.broadcasted_iota(jnp.int32, shape, 0 if flipped else 1)
    bits = blocks.bit_length() - 1
    same = (packed >> 3 == (compact & (blocks - 1))) & ((packed & 7) + shift == compact >> bits)
    return jnp.where(same, 1.0, 0.0).astype(BF16)


def unpack_rows(tiles, blocks):
    groups = [None] * 14
    for shift, tile, group in SHIFTS:
        pairs = pairs_of(tile, group)
        stacked = jnp.concatenate([tiles[k] for k, _ in pairs], axis=1)
        rows = dot(chosen_rows(blocks, shift, False), stacked, ((1,), (0,)))
        for n, (k, g) in enumerate(pairs):
            part = rows[:, n * 128 : (n + 1) * 128]
            groups[g] = part if groups[g] is None else groups[g] + part
    return groups


def repack_rows(groups, blocks):
    tiles = [None] * TILES
    for shift, tile, group in SHIFTS:
        pairs = pairs_of(tile, group)
        stacked = jnp.concatenate([groups[g] for _, g in pairs], axis=1)
        rows = dot(chosen_rows(blocks, shift, True), stacked, ((1,), (0,)))
        for n, (k, g) in enumerate(pairs):
            part = rows[:, n * 128 : (n + 1) * 128]
            tiles[k] = part if tiles[k] is None else tiles[k] + part
    return jnp.concatenate([t.reshape(blocks, 8, 128) for t in tiles], axis=1)


def combine_rows(rank, gate, tiles):
    experts, tokens = rank.shape
    rank3 = jnp.broadcast_to(rank[:, None, :], (experts, 8, tokens))
    gate2 = jnp.broadcast_to(gate[:, None, :], (experts, 8, tokens)).reshape(experts * 8, tokens)
    groups = [None] * 14

    def add(g, part):
        groups[g] = part if groups[g] is None else groups[g] + part

    for shift, tile, group in SHIFTS:
        pairs = pairs_of(tile, group)
        onehot = placed(rank3, shift)
        weight = onehot * gate2
        high = weight.astype(BF16)
        low = (weight - high.astype(F32)).astype(BF16)
        for scaled in (True, False):
            some = [(k, g) for k, g in pairs if (g < 7) == scaled]
            stacked = jnp.concatenate([tiles[k] for k, _ in some], axis=1)
            if scaled:
                sums = dot(stacked, high, ((0,), (0,))) + dot(stacked, low, ((0,), (0,)))
            else:
                sums = dot(stacked, onehot.astype(BF16), ((0,), (0,)))
            for n, (_, g) in enumerate(some):
                add(g, sums[n * 128 : (n + 1) * 128])
    return jnp.concatenate(groups[:7], axis=0), jnp.concatenate(groups[7:], axis=0)


def route_kernel(core_ref, ids_ref, gates_ref, rank_ref, gate_ref):
    core = core_ref[0, 0].astype(F32)
    rank_ref[...], gate_ref[...] = route(ids_ref[...], gates_ref[...], core, rank_ref.shape[0])


def send_kernel(rank_ref, gate_ref, own_ref, other_ref, *out_refs):
    half = own_ref.shape[0] // 2
    feats = jnp.concatenate(
        [own_ref[:half, :], other_ref[:half, :], own_ref[half:, :], other_ref[half:, :]], axis=0
    )
    source = [feats[g * 128 : (g + 1) * 128] for g in range(14)]
    rows = pack_rows(rank_ref[...], gate_ref[...], source)
    start = 0
    for ref in out_refs:
        ref[...] = rows[:, start : start + ref.shape[1]].astype(BF16)
        start += ref.shape[1]


def up_kernel(up_own, up_other, down_own, down_other, *refs):
    *recv, out_ref, x_ref, dy_ref = refs
    tiles = [tile for ref in recv for tile in split_tiles(ref[...])]
    groups = unpack_rows(tiles, recv[0].shape[0])
    for g in range(7):
        x_ref[:, g * 128 : (g + 1) * 128] = groups[g].astype(BF16)
        dy_ref[:, g * 128 : (g + 1) * 128] = groups[7 + g].astype(BF16)
    rows = x_ref.shape[0]
    block = out_ref.shape[2]
    for q in range(out_ref.shape[0]):
        units = slice(q * block, (q + 1) * block)
        up = jnp.concatenate([up_own[:, units], up_other[:, units]], axis=0)
        down = jnp.concatenate([down_own[:, units], down_other[:, units]], axis=0)
        out_ref[q, :rows, :] = dot(x_ref[...], up, ((1,), (0,))).astype(BF16)
        out_ref[q, rows:, :] = dot(dy_ref[...], down, ((1,), (0,))).astype(BF16)


def act_kernel(parts_ref, out_ref):
    summed = jnp.sum(parts_ref[...].astype(F32), axis=0)
    pre = summed[0]
    dhid = summed[1]
    sigma = 1.0 / (1.0 + jnp.exp(-pre))
    hidden = (pre * sigma).astype(BF16)
    dpre = (dhid * sigma * (1.0 + pre * (1.0 - sigma))).astype(BF16)
    for q in range(out_ref.shape[0]):
        out_ref[q, 0] = hidden
        out_ref[q, 1] = dpre


def down_kernel(recv_ref, up_own, up_other, down_own, down_other, out_ref):
    chips, rows, _ = recv_ref.shape
    half = rows // 2
    features = up_own.shape[0]
    even = features // 128 * 128
    odd = features - even
    groups = []
    for first, own, other in ((0, down_own, down_other), (half, up_own, up_other)):
        acts = jnp.concatenate([recv_ref[q, first : first + half, :] for q in range(chips)], axis=1)
        between = jnp.concatenate([own[even:, :], other[: 128 - odd, :]], axis=0)
        for weight in (own[:even, :], between, other[128 - odd :, :]):
            out = dot(acts, weight, ((1,), (1,))).astype(BF16)
            groups += [out[:, n : n + 128] for n in range(0, out.shape[1], 128)]
    out_ref[...] = repack_rows(groups, out_ref.shape[0]).astype(BF16)


def combine_kernel(rank_ref, gate_ref, recv_ref, mixed_ref, grad_ref, other_ref):
    mixed, grad = combine_rows(rank_ref[...], gate_ref[...], split_tiles(recv_ref[...]))
    width = mixed_ref.shape[0]
    mixed_ref[...] = mixed[:width]
    grad_ref[...] = grad[:width]
    other_ref[0] = mixed[width:].astype(BF16)
    other_ref[1] = grad[width:].astype(BF16)


def in_vmem(kernel, name, outs, operands, scratch=()):
    vmem = pl.BlockSpec(memory_space=pltpu.VMEM)
    scalar = pl.BlockSpec(memory_space=pltpu.SMEM)
    return pl.pallas_call(
        kernel,
        out_shape=outs,
        in_specs=[scalar if x.size == 1 else vmem for x in operands],
        out_specs=jax.tree.map(lambda _: vmem, outs),
        scratch_shapes=list(scratch),
        compiler_params=pltpu.CompilerParams(vmem_limit_bytes=16 * 1024 * 1024),
        name=name,
    )(*operands)


def local(tokens, grad_out, expert_ids, route_weight, up_weight, down_weight):
    tok_count, features = tokens.shape
    experts = lax.axis_size("expert")
    sections = lax.axis_size("section")
    chips = sections // 2
    hidden_units = up_weight.shape[2]
    block = hidden_units // chips
    rows = experts * HALF
    swap = [(s, s ^ 1) for s in range(sections)]
    same_core = [[2 * q + c for q in range(chips)] for c in range(2)]
    core = (lax.axis_index("section") & 1).astype(jnp.int32).reshape(1, 1)
    message = jax.ShapeDtypeStruct((experts, 8 * TILES, 128), BF16)
    by_expert = jax.ShapeDtypeStruct((experts, tok_count), F32)
    parts_type = jax.ShapeDtypeStruct((chips, 2 * rows, block), BF16)

    def across_experts(x):
        return lax.all_to_all(x, "expert", split_axis=0, concat_axis=0, tiled=True)

    def across_chips(x):
        return lax.all_to_all(
            x, "section", split_axis=0, concat_axis=0, axis_index_groups=same_core, tiled=True
        )

    own = jnp.concatenate([tokens.T, grad_out.T], axis=0)
    other = lax.ppermute(own, "section", swap)
    rank, gate = in_vmem(
        route_kernel, "route", (by_expert, by_expert), (core, expert_ids.T, route_weight.T)
    )
    up_own, down_own = up_weight[0], down_weight[0].T
    up_other = lax.ppermute(up_own, "section", swap)
    down_other = lax.ppermute(down_own, "section", swap)

    weights = (up_own, up_other, down_own, down_other)
    steps = 4
    act_spec = pl.BlockSpec((chips, 2, rows // steps, block), lambda i: (0, 0, i, 0))
    own_sum = jax.ShapeDtypeStruct((features, tok_count), F32)
    sums = (own_sum, own_sum, jax.ShapeDtypeStruct((2, features, tok_count), BF16))

    def layer(lead, rank, gate, own, other, *weights):
        cuts = [0, lead, 8 * TILES] if lead else [0, 8 * TILES]
        kinds = tuple(
            jax.ShapeDtypeStruct((experts, stop - start, 128), BF16) for start, stop in zip(cuts, cuts[1:])
        )
        recv = [across_experts(x) for x in in_vmem(send_kernel, "send_rows", kinds, (rank, gate, own, other))]
        parts = in_vmem(
            up_kernel,
            "up_products",
            parts_type,
            (*weights, *recv),
            [pltpu.VMEM((rows, 2 * features), BF16)] * 2,
        )
        acts = pl.pallas_call(
            act_kernel,
            grid=(steps,),
            out_shape=jax.ShapeDtypeStruct((chips, 2, rows, block), BF16),
            in_specs=[act_spec],
            out_specs=act_spec,
            compiler_params=pltpu.CompilerParams(vmem_limit_bytes=16 * 1024 * 1024),
            name="activations",
        )(across_chips(parts).reshape(chips, 2, rows, block))
        acts = across_chips(acts.reshape(chips, 2 * rows, block))
        back = across_experts(in_vmem(down_kernel, "down_products", message, (acts, *weights)))
        return in_vmem(combine_kernel, "combine_rows", sums, (rank, gate, back))

    mixed, grad, rest = lax.cond(
        core[0, 0] == 0,
        functools.partial(layer, 0),
        functools.partial(layer, LEAD),
        rank,
        gate,
        own,
        other,
        *weights,
    )
    rest = lax.ppermute(rest, "section", swap).astype(F32)
    return (mixed + rest[0]).astype(BF16).T, (grad + rest[1]).astype(BF16).T


def solution(mesh):
    return jax.shard_map(
        local,
        mesh=mesh,
        in_specs=(
            P("expert", "section"),
            P("expert", "section"),
            P("expert", None),
            P("expert", None),
            P("expert", "section", None),
            P("expert", None, "section"),
        ),
        out_specs=(P("expert", "section"), P("expert", "section")),
        check_vma=False,
    )
```

```python
import functools

import jax
import jax.numpy as jnp
from jax import lax
from jax.experimental import pallas as pl
from jax.experimental.pallas import tpu as pltpu
from jax.sharding import PartitionSpec as P

CAP = 12
LEAD = 8
HALF = CAP // 2
TILES = 11
SHIFTS = ((0, 0, 0), (-6, 0, 1), (2, 1, 1), (-4, 1, 2), (4, 2, 2), (-2, 2, 3))
F32 = jnp.float32
BF16 = jnp.bfloat16


def pairs_of(first_tile, first_group):
    return [
        (first_tile + 3 * n, first_group + 4 * n)
        for n in range(4)
        if first_tile + 3 * n < TILES and first_group + 4 * n < 14
    ]


def dot(a, b, contract):
    return lax.dot_general(a, b, ((contract[0], contract[1]), ((), ())), preferred_element_type=F32)


def placed(rank3, shift):
    experts, _, tokens = rank3.shape
    row = lax.broadcasted_iota(jnp.int32, rank3.shape, 1).astype(F32) + float(shift)
    return jnp.where(rank3 == row, 1.0, 0.0).reshape(experts * 8, tokens)


def route(ids, gates, core, experts):
    tokens = ids.shape[1]
    expert_row = lax.broadcasted_iota(jnp.int32, (experts, tokens), 0)
    named = jnp.zeros((experts, tokens), F32)
    gate = jnp.zeros((experts, tokens), F32)
    for k in range(ids.shape[0]):
        hit = ids[k : k + 1, :] == expert_row
        named = named + jnp.where(hit, 1.0, 0.0)
        gate = gate + jnp.where(hit, gates[k : k + 1, :], 0.0)
    earlier = lax.broadcasted_iota(jnp.int32, (tokens, tokens), 0) < lax.broadcasted_iota(
        jnp.int32, (tokens, tokens), 1
    )
    before = dot(named.astype(BF16), jnp.where(earlier, 1.0, 0.0).astype(BF16), ((1,), (0,)))
    rank = before - core * float(HALF)
    kept = (named > 0.5) & (rank > -0.5) & (rank < HALF - 0.5)
    return jnp.where(kept, rank, -100.0), gate


def pack_rows(rank, gate, source):
    experts, tokens = rank.shape
    rank3 = jnp.broadcast_to(rank[:, None, :], (experts, 8, tokens))
    gate2 = jnp.broadcast_to(gate[:, None, :], (experts, 8, tokens)).reshape(experts * 8, tokens)
    tiles = [None] * TILES
    for shift, tile, group in SHIFTS:
        pairs = pairs_of(tile, group)
        onehot = placed(rank3, shift)
        weight = jnp.sum(onehot * gate2, axis=1, keepdims=True)
        stacked = jnp.concatenate([source[g] for _, g in pairs], axis=0)
        rows = dot(onehot.astype(BF16), stacked, ((1,), (1,)))
        for n, (k, g) in enumerate(pairs):
            part = rows[:, n * 128 : (n + 1) * 128]
            part = part if g < 7 else part * weight
            tiles[k] = part if tiles[k] is None else tiles[k] + part
    return jnp.concatenate([t.reshape(experts, 8, 128) for t in tiles], axis=1)


def split_tiles(message):
    blocks, rows, _ = message.shape
    wide = message.astype(F32).reshape(blocks, rows // 8, 8, 128)
    return [wide[:, k].reshape(blocks * 8, 128).astype(BF16) for k in range(rows // 8)]


def chosen_rows(blocks, shift, flipped):
    shape = (blocks * 8, blocks * HALF) if flipped else (blocks * HALF, blocks * 8)
    compact = lax.broadcasted_iota(jnp.int32, shape, 1 if flipped else 0)
    packed = lax.broadcasted_iota(jnp.int32, shape, 0 if flipped else 1)
    bits = blocks.bit_length() - 1
    same = (packed >> 3 == (compact & (blocks - 1))) & ((packed & 7) + shift == compact >> bits)
    return jnp.where(same, 1.0, 0.0).astype(BF16)


def unpack_rows(tiles, blocks):
    groups = [None] * 14
    for shift, tile, group in SHIFTS:
        pairs = pairs_of(tile, group)
        stacked = jnp.concatenate([tiles[k] for k, _ in pairs], axis=1)
        rows = dot(chosen_rows(blocks, shift, False), stacked, ((1,), (0,)))
        for n, (k, g) in enumerate(pairs):
            part = rows[:, n * 128 : (n + 1) * 128]
            groups[g] = part if groups[g] is None else groups[g] + part
    return groups


def repack_rows(groups, blocks):
    tiles = [None] * TILES
    for shift, tile, group in SHIFTS:
        pairs = pairs_of(tile, group)
        stacked = jnp.concatenate([groups[g] for _, g in pairs], axis=1)
        rows = dot(chosen_rows(blocks, shift, True), stacked, ((1,), (0,)))
        for n, (k, g) in enumerate(pairs):
            part = rows[:, n * 128 : (n + 1) * 128]
            tiles[k] = part if tiles[k] is None else tiles[k] + part
    return jnp.concatenate([t.reshape(blocks, 8, 128) for t in tiles], axis=1)


def combine_rows(rank, gate, tiles, start, stop):
    experts, tokens = rank.shape
    rank3 = jnp.broadcast_to(rank[:, None, :], (experts, 8, tokens))
    gate2 = jnp.broadcast_to(gate[:, None, :], (experts, 8, tokens)).reshape(experts * 8, tokens)
    used = range(start // 128, (stop + 127) // 128)
    groups = [None] * 14

    def add(g, part):
        groups[g] = part if groups[g] is None else groups[g] + part

    for shift, tile, group in SHIFTS:
        pairs = [(k, g) for k, g in pairs_of(tile, group) if g % 7 in used]
        onehot = placed(rank3, shift)
        weight = onehot * gate2
        high = weight.astype(BF16)
        low = (weight - high.astype(F32)).astype(BF16)
        for scaled in (True, False):
            some = [(k, g) for k, g in pairs if (g < 7) == scaled]
            if not some:
                continue
            stacked = jnp.concatenate([tiles[k] for k, _ in some], axis=1)
            if scaled:
                sums = dot(stacked, high, ((0,), (0,))) + dot(stacked, low, ((0,), (0,)))
            else:
                sums = dot(stacked, onehot.astype(BF16), ((0,), (0,)))
            for n, (_, g) in enumerate(some):
                add(g, sums[n * 128 : (n + 1) * 128])
    first = used[0] * 128
    joined = (jnp.concatenate([groups[half + j] for j in used], axis=0) for half in (0, 7))
    return tuple(x[start - first : stop - first] for x in joined)


def route_kernel(core_ref, ids_ref, gates_ref, rank_ref, gate_ref):
    core = core_ref[0, 0].astype(F32)
    rank_ref[...], gate_ref[...] = route(ids_ref[...], gates_ref[...], core, rank_ref.shape[0])


def send_kernel(rank_ref, gate_ref, own_ref, other_ref, *out_refs):
    half = own_ref.shape[0] // 2
    feats = jnp.concatenate(
        [own_ref[:half, :], other_ref[:half, :], own_ref[half:, :], other_ref[half:, :]], axis=0
    )
    source = [feats[g * 128 : (g + 1) * 128] for g in range(14)]
    rows = pack_rows(rank_ref[...], gate_ref[...], source)
    start = 0
    for ref in out_refs:
        ref[...] = rows[:, start : start + ref.shape[1]].astype(BF16)
        start += ref.shape[1]


def up_kernel(up_own, up_other, down_own, down_other, *refs):
    *recv, out_ref, x_ref, dy_ref = refs
    tiles = [tile for ref in recv for tile in split_tiles(ref[...])]
    groups = unpack_rows(tiles, recv[0].shape[0])
    for g in range(7):
        x_ref[:, g * 128 : (g + 1) * 128] = groups[g].astype(BF16)
        dy_ref[:, g * 128 : (g + 1) * 128] = groups[7 + g].astype(BF16)
    rows = x_ref.shape[0]
    block = out_ref.shape[2]
    for q in range(out_ref.shape[0]):
        units = slice(q * block, (q + 1) * block)
        up = jnp.concatenate([up_own[:, units], up_other[:, units]], axis=0)
        down = jnp.concatenate([down_own[:, units], down_other[:, units]], axis=0)
        out_ref[q, :rows, :] = dot(x_ref[...], up, ((1,), (0,))).astype(BF16)
        out_ref[q, rows:, :] = dot(dy_ref[...], down, ((1,), (0,))).astype(BF16)


def act_kernel(parts_ref, out_ref):
    summed = jnp.sum(parts_ref[...].astype(F32), axis=0)
    pre = summed[0]
    dhid = summed[1]
    sigma = 1.0 / (1.0 + jnp.exp(-pre))
    hidden = (pre * sigma).astype(BF16)
    dpre = (dhid * sigma * (1.0 + pre * (1.0 - sigma))).astype(BF16)
    for q in range(out_ref.shape[0]):
        out_ref[q, 0] = hidden
        out_ref[q, 1] = dpre


def down_kernel(recv_ref, up_own, up_other, down_own, down_other, out_ref):
    chips, rows, _ = recv_ref.shape
    half = rows // 2
    features = up_own.shape[0]
    even = features // 128 * 128
    odd = features - even
    groups = []
    for first, own, other in ((0, down_own, down_other), (half, up_own, up_other)):
        acts = jnp.concatenate([recv_ref[q, first : first + half, :] for q in range(chips)], axis=1)
        between = jnp.concatenate([own[even:, :], other[: 128 - odd, :]], axis=0)
        for weight in (own[:even, :], between, other[128 - odd :, :]):
            out = dot(acts, weight, ((1,), (1,))).astype(BF16)
            groups += [out[:, n : n + 128] for n in range(0, out.shape[1], 128)]
    out_ref[...] = repack_rows(groups, out_ref.shape[0]).astype(BF16)


def combine_own_kernel(rank_ref, gate_ref, recv_ref, mixed_ref, grad_ref):
    width = mixed_ref.shape[0]
    mixed, grad = combine_rows(rank_ref[...], gate_ref[...], split_tiles(recv_ref[...]), 0, width)
    mixed_ref[...] = mixed
    grad_ref[...] = grad


def combine_other_kernel(rank_ref, gate_ref, recv_ref, out_ref):
    width = out_ref.shape[1]
    sums = combine_rows(rank_ref[...], gate_ref[...], split_tiles(recv_ref[...]), width, 2 * width)
    for n in range(2):
        out_ref[n] = sums[n].astype(BF16)


def in_vmem(kernel, name, outs, operands, scratch=()):
    vmem = pl.BlockSpec(memory_space=pltpu.VMEM)
    scalar = pl.BlockSpec(memory_space=pltpu.SMEM)
    return pl.pallas_call(
        kernel,
        out_shape=outs,
        in_specs=[scalar if x.size == 1 else vmem for x in operands],
        out_specs=jax.tree.map(lambda _: vmem, outs),
        scratch_shapes=list(scratch),
        compiler_params=pltpu.CompilerParams(vmem_limit_bytes=16 * 1024 * 1024),
        name=name,
    )(*operands)


def local(tokens, grad_out, expert_ids, route_weight, up_weight, down_weight):
    tok_count, features = tokens.shape
    experts = lax.axis_size("expert")
    sections = lax.axis_size("section")
    chips = sections // 2
    hidden_units = up_weight.shape[2]
    block = hidden_units // chips
    rows = experts * HALF
    swap = [(s, s ^ 1) for s in range(sections)]
    same_core = [[2 * q + c for q in range(chips)] for c in range(2)]
    core = (lax.axis_index("section") & 1).astype(jnp.int32).reshape(1, 1)
    message = jax.ShapeDtypeStruct((experts, 8 * TILES, 128), BF16)
    by_expert = jax.ShapeDtypeStruct((experts, tok_count), F32)
    parts_type = jax.ShapeDtypeStruct((chips, 2 * rows, block), BF16)

    def across_experts(x):
        return lax.all_to_all(x, "expert", split_axis=0, concat_axis=0, tiled=True)

    def across_chips(x):
        return lax.all_to_all(
            x, "section", split_axis=0, concat_axis=0, axis_index_groups=same_core, tiled=True
        )

    own = jnp.concatenate([tokens.T, grad_out.T], axis=0)
    other = lax.ppermute(own, "section", swap)
    rank, gate = in_vmem(
        route_kernel, "route", (by_expert, by_expert), (core, expert_ids.T, route_weight.T)
    )
    up_own, down_own = up_weight[0], down_weight[0].T
    up_other = lax.ppermute(up_own, "section", swap)
    down_other = lax.ppermute(down_own, "section", swap)

    weights = (up_own, up_other, down_own, down_other)
    steps = 4
    act_spec = pl.BlockSpec((chips, 2, rows // steps, block), lambda i: (0, 0, i, 0))
    own_sum = jax.ShapeDtypeStruct((features, tok_count), F32)
    sums = jax.ShapeDtypeStruct((2, features, tok_count), BF16)

    def layer(lead, rank, gate, own, other, *weights):
        cuts = [0, lead, 8 * TILES] if lead else [0, 8 * TILES]
        kinds = tuple(
            jax.ShapeDtypeStruct((experts, stop - start, 128), BF16) for start, stop in zip(cuts, cuts[1:])
        )
        recv = [across_experts(x) for x in in_vmem(send_kernel, "send_rows", kinds, (rank, gate, own, other))]
        parts = in_vmem(
            up_kernel,
            "up_products",
            parts_type,
            (*weights, *recv),
            [pltpu.VMEM((rows, 2 * features), BF16)] * 2,
        )
        acts = pl.pallas_call(
            act_kernel,
            grid=(steps,),
            out_shape=jax.ShapeDtypeStruct((chips, 2, rows, block), BF16),
            in_specs=[act_spec],
            out_specs=act_spec,
            compiler_params=pltpu.CompilerParams(vmem_limit_bytes=16 * 1024 * 1024),
            name="activations",
        )(across_chips(parts).reshape(chips, 2, rows, block))
        acts = across_chips(acts.reshape(chips, 2 * rows, block))
        return across_experts(in_vmem(down_kernel, "down_products", message, (acts, *weights)))

    back = lax.cond(
        core[0, 0] == 0,
        functools.partial(layer, 0),
        functools.partial(layer, LEAD),
        rank,
        gate,
        own,
        other,
        *weights,
    )
    shares = (rank, gate, back)
    rest = lax.ppermute(in_vmem(combine_other_kernel, "combine_other", sums, shares), "section", swap).astype(F32)
    mixed, grad = in_vmem(combine_own_kernel, "combine_own", (own_sum, own_sum), shares)
    return (mixed + rest[0]).astype(BF16).T, (grad + rest[1]).astype(BF16).T


def solution(mesh):
    return jax.shard_map(
        local,
        mesh=mesh,
        in_specs=(
            P("expert", "section"),
            P("expert", "section"),
            P("expert", None),
            P("expert", None),
            P("expert", "section", None),
            P("expert", None, "section"),
        ),
        out_specs=(P("expert", "section"), P("expert", "section")),
        check_vma=False,
    )
```

```python
import functools

import jax
import jax.numpy as jnp
from jax import lax
from jax.experimental import pallas as pl
from jax.experimental.pallas import tpu as pltpu
from jax.sharding import PartitionSpec as P

CAP = 12
LEAD = 8
HALF = CAP // 2
TILES = 11
SHIFTS = ((0, 0, 0), (-6, 0, 1), (2, 1, 1), (-4, 1, 2), (4, 2, 2), (-2, 2, 3))
F32 = jnp.float32
BF16 = jnp.bfloat16


def pairs_of(first_tile, first_group):
    return [
        (first_tile + 3 * n, first_group + 4 * n)
        for n in range(4)
        if first_tile + 3 * n < TILES and first_group + 4 * n < 14
    ]


def dot(a, b, contract):
    return lax.dot_general(a, b, ((contract[0], contract[1]), ((), ())), preferred_element_type=F32)


def placed(rank3, shift):
    experts, _, tokens = rank3.shape
    row = lax.broadcasted_iota(jnp.int32, rank3.shape, 1).astype(F32) + float(shift)
    return jnp.where(rank3 == row, 1.0, 0.0).reshape(experts * 8, tokens)


def route(ids, gates, core, experts):
    tokens = ids.shape[1]
    expert_row = lax.broadcasted_iota(jnp.int32, (experts, tokens), 0)
    named = jnp.zeros((experts, tokens), F32)
    gate = jnp.zeros((experts, tokens), F32)
    for k in range(ids.shape[0]):
        hit = ids[k : k + 1, :] == expert_row
        named = named + jnp.where(hit, 1.0, 0.0)
        gate = gate + jnp.where(hit, gates[k : k + 1, :], 0.0)
    earlier = lax.broadcasted_iota(jnp.int32, (tokens, tokens), 0) < lax.broadcasted_iota(
        jnp.int32, (tokens, tokens), 1
    )
    before = dot(named.astype(BF16), jnp.where(earlier, 1.0, 0.0).astype(BF16), ((1,), (0,)))
    rank = before - core * float(HALF)
    kept = (named > 0.5) & (rank > -0.5) & (rank < HALF - 0.5)
    return jnp.where(kept, rank, -100.0), gate


def pack_rows(rank, gate, source):
    experts, tokens = rank.shape
    rank3 = jnp.broadcast_to(rank[:, None, :], (experts, 8, tokens))
    gate2 = jnp.broadcast_to(gate[:, None, :], (experts, 8, tokens)).reshape(experts * 8, tokens)
    tiles = [None] * TILES
    for shift, tile, group in SHIFTS:
        pairs = pairs_of(tile, group)
        onehot = placed(rank3, shift)
        weight = jnp.sum(onehot * gate2, axis=1, keepdims=True)
        stacked = jnp.concatenate([source[g] for _, g in pairs], axis=0)
        rows = dot(onehot.astype(BF16), stacked, ((1,), (1,)))
        for n, (k, g) in enumerate(pairs):
            part = rows[:, n * 128 : (n + 1) * 128]
            part = part if g < 7 else part * weight
            tiles[k] = part if tiles[k] is None else tiles[k] + part
    return jnp.concatenate([t.reshape(experts, 8, 128) for t in tiles], axis=1)


def split_tiles(message):
    blocks, rows, _ = message.shape
    wide = message.astype(F32).reshape(blocks, rows // 8, 8, 128)
    return [wide[:, k].reshape(blocks * 8, 128).astype(BF16) for k in range(rows // 8)]


def chosen_rows(blocks, shift, flipped):
    shape = (blocks * 8, blocks * HALF) if flipped else (blocks * HALF, blocks * 8)
    compact = lax.broadcasted_iota(jnp.int32, shape, 1 if flipped else 0)
    packed = lax.broadcasted_iota(jnp.int32, shape, 0 if flipped else 1)
    bits = blocks.bit_length() - 1
    same = (packed >> 3 == (compact & (blocks - 1))) & ((packed & 7) + shift == compact >> bits)
    return jnp.where(same, 1.0, 0.0).astype(BF16)


def unpack_rows(tiles, blocks):
    groups = [None] * 14
    for shift, tile, group in SHIFTS:
        pairs = pairs_of(tile, group)
        stacked = jnp.concatenate([tiles[k] for k, _ in pairs], axis=1)
        rows = dot(chosen_rows(blocks, shift, False), stacked, ((1,), (0,)))
        for n, (k, g) in enumerate(pairs):
            part = rows[:, n * 128 : (n + 1) * 128]
            groups[g] = part if groups[g] is None else groups[g] + part
    return groups


def repack_rows(groups, blocks):
    tiles = [None] * TILES
    for shift, tile, group in SHIFTS:
        pairs = pairs_of(tile, group)
        stacked = jnp.concatenate([groups[g] for _, g in pairs], axis=1)
        rows = dot(chosen_rows(blocks, shift, True), stacked, ((1,), (0,)))
        for n, (k, g) in enumerate(pairs):
            part = rows[:, n * 128 : (n + 1) * 128]
            tiles[k] = part if tiles[k] is None else tiles[k] + part
    return jnp.concatenate([t.reshape(blocks, 8, 128) for t in tiles], axis=1)


def combine_rows(rank, gate, tiles, start, stop):
    experts, tokens = rank.shape
    rank3 = jnp.broadcast_to(rank[:, None, :], (experts, 8, tokens))
    gate2 = jnp.broadcast_to(gate[:, None, :], (experts, 8, tokens)).reshape(experts * 8, tokens)
    used = range(start // 128, (stop + 127) // 128)
    groups = [None] * 14

    def add(g, part):
        groups[g] = part if groups[g] is None else groups[g] + part

    for shift, tile, group in SHIFTS:
        pairs = [(k, g) for k, g in pairs_of(tile, group) if g % 7 in used]
        onehot = placed(rank3, shift)
        weight = onehot * gate2
        high = weight.astype(BF16)
        low = (weight - high.astype(F32)).astype(BF16)
        for scaled in (True, False):
            some = [(k, g) for k, g in pairs if (g < 7) == scaled]
            if not some:
                continue
            stacked = jnp.concatenate([tiles[k] for k, _ in some], axis=1)
            if scaled:
                sums = dot(stacked, high, ((0,), (0,))) + dot(stacked, low, ((0,), (0,)))
            else:
                sums = dot(stacked, onehot.astype(BF16), ((0,), (0,)))
            for n, (_, g) in enumerate(some):
                add(g, sums[n * 128 : (n + 1) * 128])
    first = used[0] * 128
    joined = (jnp.concatenate([groups[half + j] for j in used], axis=0) for half in (0, 7))
    return tuple(x[start - first : stop - first] for x in joined)


def route_kernel(core_ref, ids_ref, gates_ref, rank_ref, gate_ref):
    core = core_ref[0, 0].astype(F32)
    rank_ref[...], gate_ref[...] = route(ids_ref[...], gates_ref[...], core, rank_ref.shape[0])


def send_kernel(rank_ref, gate_ref, own_ref, other_ref, *out_refs):
    half = own_ref.shape[0] // 2
    feats = jnp.concatenate(
        [own_ref[:half, :], other_ref[:half, :], own_ref[half:, :], other_ref[half:, :]], axis=0
    )
    source = [feats[g * 128 : (g + 1) * 128] for g in range(14)]
    rows = pack_rows(rank_ref[...], gate_ref[...], source)
    start = 0
    for ref in out_refs:
        ref[...] = rows[:, start : start + ref.shape[1]].astype(BF16)
        start += ref.shape[1]


def up_kernel(up_own, up_other, down_own, down_other, *refs):
    *recv, out_ref, x_ref, dy_ref = refs
    tiles = [tile for ref in recv for tile in split_tiles(ref[...])]
    groups = unpack_rows(tiles, recv[0].shape[0])
    for g in range(7):
        x_ref[:, g * 128 : (g + 1) * 128] = groups[g].astype(BF16)
        dy_ref[:, g * 128 : (g + 1) * 128] = groups[7 + g].astype(BF16)
    rows = x_ref.shape[0]
    block = out_ref.shape[2]
    for q in range(out_ref.shape[0]):
        units = slice(q * block, (q + 1) * block)
        up = jnp.concatenate([up_own[:, units], up_other[:, units]], axis=0)
        down = jnp.concatenate([down_own[:, units], down_other[:, units]], axis=0)
        out_ref[q, :rows, :] = dot(x_ref[...], up, ((1,), (0,))).astype(BF16)
        out_ref[q, rows:, :] = dot(dy_ref[...], down, ((1,), (0,))).astype(BF16)


def act_kernel(parts_ref, out_ref):
    summed = jnp.sum(parts_ref[...].astype(F32), axis=0)
    pre = summed[0]
    dhid = summed[1]
    sigma = 1.0 / (1.0 + jnp.exp(-pre))
    hidden = (pre * sigma).astype(BF16)
    dpre = (dhid * sigma * (1.0 + pre * (1.0 - sigma))).astype(BF16)
    for q in range(out_ref.shape[0]):
        out_ref[q, 0] = hidden
        out_ref[q, 1] = dpre


def down_kernel(recv_ref, up_own, up_other, down_own, down_other, out_ref):
    chips, rows, _ = recv_ref.shape
    half = rows // 2
    features = up_own.shape[0]
    even = features // 128 * 128
    odd = features - even
    groups = []
    for first, own, other in ((0, down_own, down_other), (half, up_own, up_other)):
        acts = jnp.concatenate([recv_ref[q, first : first + half, :] for q in range(chips)], axis=1)
        between = jnp.concatenate([own[even:, :], other[: 128 - odd, :]], axis=0)
        for weight in (own[:even, :], between, other[128 - odd :, :]):
            out = dot(acts, weight, ((1,), (1,))).astype(BF16)
            groups += [out[:, n : n + 128] for n in range(0, out.shape[1], 128)]
    out_ref[...] = repack_rows(groups, out_ref.shape[0]).astype(BF16)


def combine_own_kernel(rank_ref, gate_ref, recv_ref, mixed_ref, grad_ref):
    width = mixed_ref.shape[0]
    mixed, grad = combine_rows(rank_ref[...], gate_ref[...], split_tiles(recv_ref[...]), 0, width)
    mixed_ref[...] = mixed
    grad_ref[...] = grad


def combine_other_kernel(rank_ref, gate_ref, recv_ref, out_ref):
    width = out_ref.shape[1]
    sums = combine_rows(rank_ref[...], gate_ref[...], split_tiles(recv_ref[...]), width, 2 * width)
    for n in range(2):
        out_ref[n] = sums[n].astype(BF16)


def in_vmem(kernel, name, outs, operands, scratch=()):
    vmem = pl.BlockSpec(memory_space=pltpu.VMEM)
    scalar = pl.BlockSpec(memory_space=pltpu.SMEM)
    return pl.pallas_call(
        kernel,
        out_shape=outs,
        in_specs=[scalar if x.size == 1 else vmem for x in operands],
        out_specs=jax.tree.map(lambda _: vmem, outs),
        scratch_shapes=list(scratch),
        compiler_params=pltpu.CompilerParams(vmem_limit_bytes=16 * 1024 * 1024),
        name=name,
    )(*operands)


def local(tokens, grad_out, expert_ids, route_weight, up_weight, down_weight):
    tok_count, features = tokens.shape
    experts = lax.axis_size("expert")
    sections = lax.axis_size("section")
    chips = sections // 2
    hidden_units = up_weight.shape[2]
    block = hidden_units // chips
    rows = experts * HALF
    swap = [(s, s ^ 1) for s in range(sections)]
    same_core = [[2 * q + c for q in range(chips)] for c in range(2)]
    core = (lax.axis_index("section") & 1).astype(jnp.int32).reshape(1, 1)
    message = jax.ShapeDtypeStruct((experts, 8 * TILES, 128), BF16)
    by_expert = jax.ShapeDtypeStruct((experts, tok_count), F32)
    parts_type = jax.ShapeDtypeStruct((chips, 2 * rows, block), BF16)

    def across_experts(x):
        return lax.all_to_all(x, "expert", split_axis=0, concat_axis=0, tiled=True)

    def across_chips(x):
        return lax.all_to_all(
            x, "section", split_axis=0, concat_axis=0, axis_index_groups=same_core, tiled=True
        )

    own = jnp.concatenate([tokens.T, grad_out.T], axis=0)
    other = lax.ppermute(own, "section", swap)
    rank, gate = in_vmem(
        route_kernel, "route", (by_expert, by_expert), (core, expert_ids.T, route_weight.T)
    )
    up_own, down_own = up_weight[0], down_weight[0].T
    up_other = lax.ppermute(up_own, "section", swap)
    down_other = lax.ppermute(down_own, "section", swap)

    weights = (up_own, up_other, down_own, down_other)
    own_sum = jax.ShapeDtypeStruct((features, tok_count), F32)
    sums = jax.ShapeDtypeStruct((2, features, tok_count), BF16)

    def layer(lead, rank, gate, own, other, *weights):
        cuts = [0, lead, 8 * TILES] if lead else [0, 8 * TILES]
        kinds = tuple(
            jax.ShapeDtypeStruct((experts, stop - start, 128), BF16) for start, stop in zip(cuts, cuts[1:])
        )
        recv = [across_experts(x) for x in in_vmem(send_kernel, "send_rows", kinds, (rank, gate, own, other))]
        parts = in_vmem(
            up_kernel,
            "up_products",
            parts_type,
            (*weights, *recv),
            [pltpu.VMEM((rows, 2 * features), BF16)] * 2,
        )
        kind = jax.ShapeDtypeStruct((chips, 2, rows, block), BF16)
        acts = in_vmem(act_kernel, "activations", kind, (across_chips(parts).reshape(kind.shape),))
        acts = across_chips(acts.reshape(chips, 2 * rows, block))
        return across_experts(in_vmem(down_kernel, "down_products", message, (acts, *weights)))

    back = lax.cond(
        core[0, 0] == 0,
        functools.partial(layer, 0),
        functools.partial(layer, LEAD),
        rank,
        gate,
        own,
        other,
        *weights,
    )
    shares = (rank, gate, back)
    rest = lax.ppermute(in_vmem(combine_other_kernel, "combine_other", sums, shares), "section", swap).astype(F32)
    mixed, grad = in_vmem(combine_own_kernel, "combine_own", (own_sum, own_sum), shares)
    return (mixed + rest[0]).astype(BF16).T, (grad + rest[1]).astype(BF16).T


def solution(mesh):
    return jax.shard_map(
        local,
        mesh=mesh,
        in_specs=(
            P("expert", "section"),
            P("expert", "section"),
            P("expert", None),
            P("expert", None),
            P("expert", "section", None),
            P("expert", None, "section"),
        ),
        out_specs=(P("expert", "section"), P("expert", "section")),
        check_vma=False,
    )
```
